32 devices in a mesh: groups: 2 (over x), expert: 2 (over core), cuts: 8 (over z, y).
Axes of the slice: x: 2, y: 2, z: 4, core: 2. Of those that a mesh axis runs over, the one named last changes fastest.
Arguments:
- tokens: bfloat16 [1536, 6144], P(('groups', 'expert', 'cuts')), parts along dimension 0, may hold values from -6 to 6
- top_experts: int32 [1536, 2], P(('groups', 'expert', 'cuts')), parts along dimension 0, may hold values from 0 to 7, all different within a row; in each aligned block of 48 rows (0 to 47, 48 to 95, ...) at most 18 rows name the same one
- gate_fixed: int32 [1536, 2], P(('groups', 'expert', 'cuts')), parts along dimension 0, may hold values from 1 to 65535
- w_up: bfloat16 [2, 6144, 16384], P('expert', None, 'cuts'), may hold values from -0.078125 to 0.078125
- w_down: bfloat16 [2, 16384, 6144], P('expert', 'cuts'), may hold values from -0.046875 to 0.046875
Outputs:
- mixed: bfloat16 [1536, 6144], P(('groups', 'expert', 'cuts')), parts along dimension 0
The draws below stay inside these ranges and needn't reach their ends.
There are 2 independent parts, one for each index of `groups`. The reference program is written for one: setup_inputs(seed, part) draws one part's arguments, and reference() takes and returns one part's arrays. A program takes and returns all parts, laid end to end along the dimension named above; an argument that names none is the same for every part. Nothing has to cross between parts.
Inputs may be any that keep to these rules, and one draw needn't show every extreme that they name: `top_experts`: each row names two different experts; the rows of one device name one expert at most 18 times.
All inputs are finite; a program needn't handle non-finite values.
Results may differ from the reference program's by a relative error of at most 0.0049.
Values may be sent and summed in bfloat16 or wider, within the bound.
A program may use at most 128 MiB of HBM per device.

```python
import math
import jax
import jax.numpy as jnp
import numpy as np
from jax import lax

D = 6144
FF = 16384
ROUTED = 8
ROWS_DEV = 48
EXPERTS = 2
CAP = 18
ROWS = 768


def plant(drawn, own_key, low, top_value):
    longest = drawn.shape.index(max(drawn.shape))
    spots = []
    for shift in (0, 1):
        where = [jax.random.randint(jax.random.fold_in(own_key, axis), (), 0, length) for axis, length in enumerate(drawn.shape)]
        where[longest] = (where[longest] + shift) % drawn.shape[longest]
        spots.append(tuple(where))
    return drawn.at[spots[0]].set(low).at[spots[1]].set(top_value)


def block_scale(stream_key, extent, shards, low, high):
    def one(axis_at, blocks):
        heights = jax.random.uniform(jax.random.fold_in(jax.random.fold_in(stream_key, 6), axis_at), (blocks,), jnp.float32, low / len(shards), high / len(shards))
        return jnp.repeat(jnp.exp(heights), extent[axis_at] // blocks).reshape((-1,) + (1,) * (len(extent) - axis_at - 1))

    gain = one(*shards[0])
    for cut in shards[1:]:
        gain = gain * one(*cut)
    return gain


def shared_out(own_key, own, number, rows, count, top, reach, slope):
    order = jax.random.permutation(own_key, count)
    heavy_load, usual = load_shares(count, rows * top, reach, slope, True), load_shares(count, rows * top, reach, slope, False)
    places = jnp.arange(count)

    def named(sizes, offset_by):
        used = int((sizes > 0).sum())
        fixed = max(1, used // 4)
        shifted = fixed + (places - fixed + offset_by * (used - fixed)) % max(1, count - fixed)
        return jnp.zeros((count,), jnp.int32).at[order[jnp.where(places < fixed, places, shifted)]].set(jnp.asarray(sizes, jnp.int32))

    sizes = jnp.where(number % 4 == 0, named(heavy_load, number // 4), named(usual, number - number // 4 - 1))
    mixed = jax.random.permutation(jax.random.fold_in(own, 3), count)
    donor, sink = mixed[0:count // 2 * 2:2], mixed[1:count // 2 * 2:2]
    margin = jnp.minimum(sizes[donor] - 1, reach - sizes[sink]) // 2
    margin = jnp.where((donor == order[0]) | (sink == order[0]) | (sizes[sink] == 0), 0, jnp.maximum(margin, 0))
    shifted = jax.random.randint(jax.random.fold_in(own, 4), (count // 2,), 0, 1 << 20) % (margin + 1)
    sizes = sizes.at[donor].add(-shifted).at[sink].add(shifted)
    members = jnp.searchsorted(jnp.cumsum(sizes), jnp.arange(rows * top), side="right").astype(jnp.int32)
    grid = members.reshape(top, rows).T
    grid = grid[jax.random.permutation(jax.random.fold_in(own, 1), rows)]
    offset_by = jax.random.randint(jax.random.fold_in(own, 2), (rows, 1), 0, top)
    return jnp.take_along_axis(grid, (jnp.arange(top)[None, :] + offset_by) % top, axis=1)


def load_shares(count, total, reach, slope, full):
    weights = [(1 << 20) // math.isqrt(rank ** slope) + 1 for rank in range(1, count + 1)]
    largest = reach if full else min(reach, max(-(-total // count), total * weights[0] // sum(weights)))
    least = 1 if total - largest >= count - 1 else 0
    counts, spare = [largest] + [least] * (count - 1), total - largest - least * (count - 1)
    while spare > 0:
        movable = [i for i in range(1, count) if counts[i] < largest] or [i for i in range(1, count) if counts[i] < reach]
        whole, remaining = sum([weights[i] for i in movable]), spare
        for i in movable:
            addition = min(reach - counts[i], max(1, remaining * weights[i] // whole), spare)
            counts[i] = counts[i] + addition
            spare = spare - addition
    return np.array(counts)


def normal_values(stream_key, dims, scale, most, cuts=(), dtype=jnp.bfloat16):
    level = block_scale(stream_key, dims, cuts, -0.22, 0.18) if cuts else 1.0
    array = jax.random.normal(stream_key, dims, jnp.float32) * scale * level
    return jnp.minimum(jnp.maximum(array, -most), most).astype(dtype)


def setup_inputs(seed: int = 0, part: int = 0) -> dict:
    key_of = jax.random.split(jax.random.key(seed), 6)
    part_keys = jax.random.split(jax.random.fold_in(key_of[5], part), 6)
    tokens = normal_values(part_keys[0], (ROWS, D), 1.0, 6.0, ((0, 16),))
    top_experts_keys = jax.random.split(jax.random.fold_in(part_keys[1], 1), ROWS // ROWS_DEV)
    top_experts_turns = jax.random.permutation(jax.random.fold_in(part_keys[1], 3), ROWS // ROWS_DEV)
    top_experts = jax.vmap(lambda own, number: shared_out(jax.random.fold_in(part_keys[1], 2), own, number, ROWS_DEV, ROUTED, 2, CAP, 2))(top_experts_keys, top_experts_turns).reshape((ROWS, 2))
    gate_fixed = plant(jax.random.randint(part_keys[2], (ROWS, 2), 1, 65536), jax.random.fold_in(part_keys[2], 1), 1, 65535).astype(jnp.int32)
    w_up = normal_values(key_of[3], (EXPERTS, D, FF), D ** -0.5, 0.078125, ((0, 2), (2, 8)))
    w_down = normal_values(key_of[4], (EXPERTS, FF, D), FF ** -0.5, 0.046875, ((0, 2), (1, 8)))
    return dict(tokens=tokens, top_experts=top_experts, gate_fixed=gate_fixed, w_up=w_up, w_down=w_down)


def reference(tokens, top_experts, gate_fixed, w_up, w_down):
    blocks = ROWS // ROWS_DEV
    tok_blocks = tokens.reshape(blocks, ROWS_DEV, D).astype(jnp.float32)
    top_blocks = top_experts.reshape(blocks, ROWS_DEV, 2)
    scaling = gate_fixed.reshape(blocks, ROWS_DEV, 2).astype(jnp.float32) * (1.0 / 65536.0)
    slot_ids = lax.broadcasted_iota(jnp.int32, (1, CAP, 1), 1)
    total = jnp.zeros((blocks, ROWS_DEV, D), jnp.float32)
    for expert in range(EXPERTS):
        matched = top_blocks == expert
        row_hit = jnp.any(matched, axis=2).astype(jnp.int32)
        row_gate = jnp.sum(jnp.where(matched, scaling, 0.0), axis=2)
        position = (jnp.cumsum(row_hit, axis=1) - 1).astype(jnp.int32)
        chosen = (position[:, None, :] == slot_ids) & (row_hit[:, None, :] > 0)
        slot_rows = jnp.einsum("bsr,brd->bsd", chosen.astype(jnp.float32), tok_blocks).astype(jnp.bfloat16)
        hidden = jax.nn.gelu(jnp.dot(slot_rows.reshape(blocks * CAP, D), w_up[expert], preferred_element_type=jnp.float32), approximate=True).astype(jnp.bfloat16)
        expert_out = jnp.dot(hidden, w_down[expert], preferred_element_type=jnp.float32).reshape(blocks, CAP, D)
        weighted = jnp.where(chosen, row_gate[:, None, :], 0.0)
        total = total + jnp.einsum("bsr,bsd->brd", weighted, expert_out, precision=lax.Precision.HIGHEST)
    return total.reshape(ROWS, D).astype(jnp.bfloat16)
```

```python
import functools

import jax
import jax.numpy as jnp
from jax import lax
from jax.experimental import pallas as pl
from jax.experimental.pallas import tpu as pltpu
from jax.sharding import PartitionSpec as P

F32, BF16 = jnp.float32, jnp.bfloat16
MAIN = 16
REST = 2
PARTS = 2
UPC = 256
DNC = 768
HELD = 6


def iota(shape, dim):
    return lax.broadcasted_iota(jnp.int32, shape, dim)


def kernel(
    Z, Y, half, fold,
    tok, top, gate, w_up, w_down, out,
    X, Xf, hid, wu, wd, stage, rcat, Yb, Rb, fin, fin_out,
    up_sem, dn_sem, sib_s, sib_r, ag_s, ag_r, y_s, y_r, rs_s, rs_r, fs, fr,
):
    e = lax.axis_index("expert")
    k = lax.axis_index("cuts")
    z, y = k // Y, k % Y
    devs = 2 * Z * Y
    rows = devs * MAIN
    extra = devs * REST
    nup, ndn = w_up.shape[1] // UPC, w_down.shape[1] // DNC
    per = ndn // PARTS
    folds = half // fold
    other = 1 - e

    def cup(i):
        return pltpu.make_async_copy(w_up.at[:, pl.ds(i * UPC, UPC)], wu.at[i], up_sem.at[i])

    def cdn(i):
        return pltpu.make_async_copy(
            w_down.at[:, pl.ds(i * DNC, DNC)], wd.at[i % HELD], dn_sem.at[i % HELD]
        )

    for i in range(nup):
        cup(i).start()
    for i in range(min(HELD, ndn)):
        cdn(i).start()

    barrier = pltpu.get_barrier_semaphore()
    cuts_up, cuts_down, cuts_y = (z + 1) * Y + y, (z - 1) * Y + y, z * Y + (Y - 1 - y)
    pl.semaphore_signal(barrier, inc=1, device_id={"expert": other})
    if Y == 2:
        pl.semaphore_signal(barrier, inc=1, device_id={"cuts": cuts_y})

    @pl.when(z < Z - 1)
    def _():
        pl.semaphore_signal(barrier, inc=1, device_id={"cuts": cuts_up})

    @pl.when(z > 0)
    def _():
        pl.semaphore_signal(barrier, inc=1, device_id={"cuts": cuts_down})

    n = tok.shape[0]
    tri = (iota((n, n), 0) <= iota((n, n), 1)).astype(F32).astype(BF16)
    hits, places, gates = [], [], []
    for x in range(2):
        m = (top[...] == x).astype(F32)
        hit = jnp.sum(m, axis=0, keepdims=True)
        g = jnp.sum(m * (gate[...].astype(F32) * (1.0 / 65536.0)), axis=0, keepdims=True)
        hb = jnp.broadcast_to(hit, (16, n)).astype(BF16)
        places.append(jnp.dot(hb, tri, preferred_element_type=F32)[0:1] - 1.0)
        hits.append(hit)
        gates.append(g)

    def pick(a, which):
        return jnp.where(which == 0, a[0], a[1])

    def select(which, slot):
        at = pick(places, which) == slot.astype(F32)
        return jnp.where(at & (pick(hits, which) > 0.5), 1.0, 0.0)

    ids = iota((MAIN, n), 0)
    mine = iota((MAIN, n), 0) * 0

    def fill(which, h, put):
        w = mine + which
        main = select(w, ids).astype(BF16)
        put(0, half, jnp.dot(main, tok[:, h * half:(h + 1) * half], preferred_element_type=F32).astype(BF16))
        acc = jnp.zeros((MAIN, fold), F32)
        rest = select(w, MAIN + ids // folds)
        for j in range(folds):
            sel = jnp.where(ids % folds == j, rest, 0.0).astype(BF16)
            lo = h * half + j * fold
            acc += jnp.dot(sel, tok[:, lo:lo + fold], preferred_element_type=F32)
        put(half, half + fold, acc.astype(BF16))

    def dev_of(zs, ys, c):
        return (zs * Y + ys) * 2 + c

    def sib(h):
        d = dev_of(z, y, e)
        return pltpu.make_async_remote_copy(
            stage.at[h], X.at[h, d], sib_s.at[h], sib_r.at[h], device_id={"expert": other}
        )

    def ag(d, h, dev):
        tgt = (cuts_up, cuts_down, cuts_y)[d]
        return pltpu.make_async_remote_copy(
            X.at[h, dev], X.at[h, dev], ag_s.at[d, h, dev], ag_r.at[h, dev], device_id={"cuts": tgt}
        )

    def ag_all(h, dev, act):
        @pl.when(z < Z - 1)
        def _():
            act(ag(0, h, dev))

        @pl.when(z > 0)
        def _():
            act(ag(1, h, dev))

        if Y == 2:
            act(ag(2, h, dev))

    def go(c):
        c.start()

    def sent(c):
        c.wait_send()

    own, sib_dev = dev_of(z, y, e), dev_of(z, y, other)
    for h in range(PARTS):
        def put(lo, hi, v):
            stage[h, :, lo:hi] = v

        fill(other, h, put)

    peers = 1 + (1 if Y == 2 else 0) + jnp.where(z < Z - 1, 1, 0) + jnp.where(z > 0, 1, 0)
    pl.semaphore_wait(barrier, peers)

    for h in range(PARTS):
        sib(h).start()
    for h in range(PARTS):
        def put(lo, hi, v):
            X[h, own, :, lo:hi] = v

        fill(e, h, put)
        ag_all(h, own, go)
    for h in range(PARTS):
        sib(h).wait_recv()
        ag_all(h, sib_dev, go)

    def relay(s, act, waits):
        @pl.when(z - s >= 0)
        def _():
            for h in range(PARTS):
                for c in range(2):
                    dev = dev_of(z - s, y, c)
                    if waits:
                        ag(0, h, dev).wait_recv()

                    @pl.when(z < Z - 1)
                    def _():
                        act(ag(0, h, dev))

                    if Y == 2:
                        act(ag(2, h, dev))

        @pl.when(z + s < Z)
        def _():
            for h in range(PARTS):
                for c in range(2):
                    dev = dev_of(z + s, y, c)
                    if waits:
                        ag(1, h, dev).wait_recv()

                    @pl.when(z > 0)
                    def _():
                        act(ag(1, h, dev))

                    if Y == 2:
                        act(ag(2, h, dev))

    @pl.loop(1, Z)
    def _(s):
        relay(s, go, True)

    if Y == 2:
        @pl.loop(0, Z)
        def _(zs):
            for h in range(PARTS):
                for c in range(2):
                    ag(2, h, dev_of(zs, 1 - y, c)).wait_recv()

    for h in range(PARTS):
        @pl.loop(0, devs)
        def _(d):
            Xf[pl.ds(pl.multiple_of(d * MAIN, MAIN), MAIN), h * half:(h + 1) * half] = X[h, d, :, 0:half]

    def unfold(shape, a, b):
        p, q = iota(shape, a), iota(shape, b)
        want = (q % folds) * extra + (q // MAIN) * REST + (q % MAIN) // folds
        return (p == want).astype(F32).astype(BF16)

    spread = unfold((rows, rows), 0, 1)
    for h in range(PARTS):
        got = jnp.dot(
            spread, X[h, :, :, half:].reshape(rows, fold), preferred_element_type=F32
        ).astype(BF16)
        for j in range(folds):
            lo = h * half + j * fold
            Xf[rows:, lo:lo + fold] = got[j * extra:(j + 1) * extra]

    @pl.loop(0, nup)
    def _(i):
        cup(i).wait()
        a = jnp.dot(Xf[...], wu[i], preferred_element_type=F32)
        hid[:, pl.ds(pl.multiple_of(i * UPC, UPC), UPC)] = jax.nn.gelu(a, approximate=True).astype(BF16)

    for h in range(PARTS):
        sib(h).wait_send()
        ag_all(h, own, sent)
        ag_all(h, sib_dev, sent)

    @pl.loop(1, Z)
    def _(s):
        relay(s, sent, False)

    def ycopy(h, zd, c):
        return pltpu.make_async_remote_copy(
            X.at[h, dev_of(zd, 1 - y, c)], Yb.at[h, zd, c], y_s.at[h, zd, c], y_r.at[h, zd, c],
            device_id={"cuts": cuts_y},
        )

    def rcopy(h, zd, slot, c, tgt):
        return pltpu.make_async_remote_copy(
            X.at[h, dev_of(zd, y, c)], Rb.at[h, slot, c], rs_s.at[h, slot, c], rs_r.at[h, slot, c],
            device_id={"cuts": tgt},
        )

    def far_first(act):
        @pl.loop(0, Z)
        def _(t):
            s = Z - 1 - t

            @pl.when(z + s < Z)
            def _():
                act(z + s)

            @pl.when((z - s >= 0) & (s > 0))
            def _():
                act(z - s)

    fold_in = unfold((rows, rows), 1, 0)
    for h in range(PARTS):
        @pl.loop(0, per)
        def _(t):
            i = h * per + t
            cdn(i).wait()
            a = jnp.dot(hid[...], wd[i % HELD], preferred_element_type=F32).astype(BF16)

            @pl.when(i + HELD < ndn)
            def _():
                cdn(i + HELD).start()

            X[h, :, :, pl.ds(pl.multiple_of(t * DNC, DNC), DNC)] = a[:rows].reshape(devs, MAIN, DNC)
            for j in range(DNC // fold):
                at = (t * (DNC // fold) + j) * extra
                rcat[pl.ds(pl.multiple_of(at, extra), extra), :] = a[rows:, j * fold:(j + 1) * fold]

        X[h, :, :, half:] = jnp.dot(
            fold_in, rcat[...], preferred_element_type=F32
        ).astype(BF16).reshape(devs, MAIN, fold)
        if Y == 2:
            def send_y(zd):
                for c in range(2):
                    ycopy(h, zd, c).start()

            far_first(send_y)

    def total(h, zd, c, slots):
        v = X[h, dev_of(zd, y, c)].astype(F32)
        if Y == 2:
            ycopy(h, zd, c).wait_recv()
            v += Yb[h, zd, c].astype(F32)
        return v

    def arrived(h, slot, c):
        rcopy(h, z, slot, c, cuts_up).wait_recv()
        return Rb[h, slot, c].astype(F32)

    def fcopy(h):
        return pltpu.make_async_remote_copy(
            fin_out.at[h], fin.at[h, e], fs.at[h], fr.at[h], device_id={"expert": other}
        )

    for h in range(PARTS):
        @pl.loop(0, Z - 1)
        def _(t):
            s = Z - 1 - t

            def hop(zd, slot, tgt, first):
                for c in range(2):
                    d = dev_of(zd, y, c)

                    v = total(h, zd, c, 0)

                    @pl.when(first)
                    def _():
                        X[h, d] = v.astype(BF16)

                    @pl.when(jnp.logical_not(first))
                    def _():
                        X[h, d] = (v + arrived(h, slot, c)).astype(BF16)

                    rcopy(h, zd, slot, c, tgt).start()

            @pl.when(z + s < Z)
            def _():
                hop(z + s, z + s + 1, cuts_up, z == 0)

            @pl.when(z - s >= 0)
            def _():
                hop(z - s, z - s, cuts_down, z == Z - 1)

        for which in range(2):
            c = (other, e)[which]
            dst = fin_out.at[h] if which == 0 else fin.at[h, e]
            dst[...] = total(h, z, c, 0)

            @pl.when(z > 0)
            def _():
                dst[...] += arrived(h, z + 1, c)

            @pl.when(z < Z - 1)
            def _():
                dst[...] += arrived(h, z, c)

            if which == 0:
                fcopy(h).start()

    q = iota((4 * MAIN, n), 0)
    which = (q // MAIN) % 2
    low = q < 2 * MAIN
    slot = jnp.where(low, q % MAIN, MAIN + (q % MAIN) // folds)
    weight = select(which, slot) * pick(gates, which)
    for h in range(PARTS):
        fcopy(h).wait()
        for j in range(folds):
            lhs = jnp.where(low | (q % folds == j), weight, 0.0)
            rhs = jnp.concatenate(
                [
                    fin[h, :, :, j * fold:(j + 1) * fold].reshape(2 * MAIN, fold),
                    fin[h, :, :, half:].reshape(2 * MAIN, fold),
                ],
                axis=0,
            )
            lo = h * half + j * fold
            out[:, lo:lo + fold] = lax.dot_general(
                lhs, rhs, (((0,), (0,)), ((), ())),
                precision=lax.Precision.HIGHEST, preferred_element_type=F32,
            ).astype(BF16)

    for h in range(PARTS):
        if Y == 2:
            @pl.loop(0, Z)
            def _(zd):
                for c in range(2):
                    ycopy(h, zd, c).wait_send()

        @pl.loop(1, Z)
        def _(s):
            @pl.when(z + s < Z)
            def _():
                for c in range(2):
                    rcopy(h, z + s, z + s + 1, c, cuts_up).wait_send()

            @pl.when(z - s >= 0)
            def _():
                for c in range(2):
                    rcopy(h, z - s, z - s, c, cuts_down).wait_send()


def body(Z, Y, tokens, top_experts, gate_fixed, w_up, w_down):
    n, width = tokens.shape
    units = w_up.shape[2]
    half = width // PARTS
    fold = half * REST // MAIN
    devs = 2 * Z * Y
    rows = devs * MAIN
    extra = devs * REST
    nup, ndn = units // UPC, width // DNC
    cols = half + fold
    DMA = pltpu.SemaphoreType.DMA
    vm = pl.BlockSpec(memory_space=pltpu.VMEM)
    anyw = pl.BlockSpec(memory_space=pl.ANY)
    return pl.pallas_call(
        functools.partial(kernel, Z, Y, half, fold),
        out_shape=jax.ShapeDtypeStruct((n, width), BF16),
        in_specs=[vm, vm, vm, anyw, anyw],
        out_specs=vm,
        scratch_shapes=[
            pltpu.VMEM((PARTS, devs, MAIN, cols), BF16),
            pltpu.VMEM((rows + extra, width), BF16),
            pltpu.VMEM((rows + extra, units), BF16),
            pltpu.VMEM((nup, width, UPC), BF16),
            pltpu.VMEM((HELD, units, DNC), BF16),
            pltpu.VMEM((PARTS, MAIN, cols), BF16),
            pltpu.VMEM((rows, fold), BF16),
            pltpu.VMEM((PARTS, Z, 2, MAIN, cols), BF16),
            pltpu.VMEM((PARTS, Z + 1, 2, MAIN, cols), BF16),
            pltpu.VMEM((PARTS, 2, MAIN, cols), F32),
            pltpu.VMEM((PARTS, MAIN, cols), F32),
            DMA((nup,)), DMA((HELD,)),
            DMA((PARTS,)), DMA((PARTS,)),
            DMA((3, PARTS, devs)), DMA((PARTS, devs)),
            DMA((PARTS, Z, 2)), DMA((PARTS, Z, 2)),
            DMA((PARTS, Z + 1, 2)), DMA((PARTS, Z + 1, 2)),
            DMA((PARTS,)), DMA((PARTS,)),
        ],
        compiler_params=pltpu.CompilerParams(
            collective_id=0, has_side_effects=True, vmem_limit_bytes=63 * 1024 * 1024
        ),
        cost_estimate=pl.CostEstimate(
            flops=4 * (rows + extra) * width * units,
            bytes_accessed=4 * width * units,
            transcendentals=(rows + extra) * units,
        ),
    )(tokens, top_experts.T, gate_fixed.T, w_up[0], w_down[0])


def solution(mesh):
    cuts = mesh.shape["cuts"]
    Y = 2 if cuts == 8 else 1
    return jax.shard_map(
        functools.partial(body, cuts // Y, Y),
        mesh=mesh,
        in_specs=(
            P(("groups", "expert", "cuts"), None),
            P(("groups", "expert", "cuts"), None),
            P(("groups", "expert", "cuts"), None),
            P("expert", None, "cuts"),
            P("expert", "cuts", None),
        ),
        out_specs=P(("groups", "expert", "cuts"), None),
        check_vma=False,
    )
```

```python
import functools

import jax
import jax.numpy as jnp
from jax import lax
from jax.experimental import pallas as pl
from jax.experimental.pallas import tpu as pltpu
from jax.sharding import PartitionSpec as P

F32, BF16 = jnp.float32, jnp.bfloat16
MAIN = 16
REST = 2
PARTS = 3
FIRST = 0
UPC = 256
DNC = 1024
HELD = 4


def iota(shape, dim):
    return lax.broadcasted_iota(jnp.int32, shape, dim)


def kernel(
    Z, Y, half, fold,
    tok, top, gate, w_up, w_down, out,
    X, Xf, acc_up, hid, wu, wd, stage, rcat, Yb, Rb, fin, fin_out,
    up_sem, dn_sem, sib_s, sib_r, ag_s, ag_r, y_s, y_r, rs_s, rs_r, fs, fr,
):
    e = lax.axis_index("expert")
    k = lax.axis_index("cuts")
    z, y = k // Y, k % Y
    devs = 2 * Z * Y
    rows = devs * MAIN
    extra = devs * REST
    nup, ndn = w_up.shape[1] // UPC, w_down.shape[1] // DNC
    per = ndn // PARTS
    folds = half // fold
    other = 1 - e

    def cup(i):
        return pltpu.make_async_copy(w_up.at[:, pl.ds(i * UPC, UPC)], wu.at[i], up_sem.at[i])

    def cdn(i):
        return pltpu.make_async_copy(
            w_down.at[:, pl.ds(i * DNC, DNC)], wd.at[i % HELD], dn_sem.at[i % HELD]
        )

    for i in range(nup):
        cup(i).start()
    for i in range(min(HELD, ndn)):
        cdn(i).start()

    barrier = pltpu.get_barrier_semaphore()
    cuts_up, cuts_down, cuts_y = (z + 1) * Y + y, (z - 1) * Y + y, z * Y + (Y - 1 - y)
    pl.semaphore_signal(barrier, inc=1, device_id={"expert": other})
    if Y == 2:
        pl.semaphore_signal(barrier, inc=1, device_id={"cuts": cuts_y})

    @pl.when(z < Z - 1)
    def _():
        pl.semaphore_signal(barrier, inc=1, device_id={"cuts": cuts_up})

    @pl.when(z > 0)
    def _():
        pl.semaphore_signal(barrier, inc=1, device_id={"cuts": cuts_down})

    n = tok.shape[0]
    tri = (iota((n, n), 0) <= iota((n, n), 1)).astype(F32).astype(BF16)
    hits, places, gates = [], [], []
    for x in range(2):
        m = (top[...] == x).astype(F32)
        hit = jnp.sum(m, axis=0, keepdims=True)
        g = jnp.sum(m * (gate[...].astype(F32) * (1.0 / 65536.0)), axis=0, keepdims=True)
        hb = jnp.broadcast_to(hit, (16, n)).astype(BF16)
        places.append(jnp.dot(hb, tri, preferred_element_type=F32)[0:1] - 1.0)
        hits.append(hit)
        gates.append(g)

    def pick(a, which):
        return jnp.where(which == 0, a[0], a[1])

    def select(which, slot):
        at = pick(places, which) == slot.astype(F32)
        return jnp.where(at & (pick(hits, which) > 0.5), 1.0, 0.0)

    ids = iota((MAIN, n), 0)
    mine = iota((MAIN, n), 0) * 0

    def fill(which, h, put):
        w = mine + which
        main = select(w, ids).astype(BF16)
        put(0, half, jnp.dot(main, tok[:, h * half:(h + 1) * half], preferred_element_type=F32).astype(BF16))
        acc = jnp.zeros((MAIN, fold), F32)
        rest = select(w, MAIN + ids // folds)
        for j in range(folds):
            sel = jnp.where(ids % folds == j, rest, 0.0).astype(BF16)
            lo = h * half + j * fold
            acc += jnp.dot(sel, tok[:, lo:lo + fold], preferred_element_type=F32)
        put(half, half + fold, acc.astype(BF16))

    def dev_of(zs, ys, c):
        return (zs * Y + ys) * 2 + c

    def sib(h):
        d = dev_of(z, y, e)
        return pltpu.make_async_remote_copy(
            stage.at[h], X.at[h, d], sib_s.at[h], sib_r.at[h], device_id={"expert": other}
        )

    def ag(d, h, dev):
        tgt = (cuts_up, cuts_down, cuts_y)[d]
        return pltpu.make_async_remote_copy(
            X.at[h, dev], X.at[h, dev], ag_s.at[d, h, dev], ag_r.at[h, dev], device_id={"cuts": tgt}
        )

    def ag_all(h, dev, act):
        @pl.when(z < Z - 1)
        def _():
            act(ag(0, h, dev))

        @pl.when(z > 0)
        def _():
            act(ag(1, h, dev))

        if Y == 2:
            act(ag(2, h, dev))

    def go(c):
        c.start()

    def sent(c):
        c.wait_send()

    own, sib_dev = dev_of(z, y, e), dev_of(z, y, other)
    early = FIRST if Y == 2 else 0

    for h in range(PARTS):
        def put(lo, hi, v):
            stage[h, :, lo:hi] = v

        fill(other, h, put)

    peers = 1 + (1 if Y == 2 else 0) + jnp.where(z < Z - 1, 1, 0) + jnp.where(z > 0, 1, 0)
    pl.semaphore_wait(barrier, peers)

    for h in range(PARTS):
        sib(h).start()
    for h in range(PARTS):
        def put(lo, hi, v):
            X[h, own, :, lo:hi] = v

        fill(e, h, put)
        ag_all(h, own, go)

    @pl.loop(0, PARTS)
    def _(h):
        sib(h).wait_recv()
        ag_all(h, sib_dev, go)

    def along(h, dev, act):
        @pl.when(z < Z - 1)
        def _():
            act(ag(0, h, dev))

        @pl.when(z > 0)
        def _():
            act(ag(1, h, dev))

    def crossed(act, waits):
        for h in range(early):
            for c in range(2):
                dev = dev_of(z, 1 - y, c)
                if waits:
                    ag(2, h, dev).wait_recv()
                along(h, dev, act)

    def relay(h, s, ys, cross, act, waits):
        for c in range(2):
            @pl.when(z - s >= 0)
            def _():
                dev = dev_of(z - s, ys, c)
                if waits:
                    ag(0, h, dev).wait_recv()

                @pl.when(z < Z - 1)
                def _():
                    act(ag(0, h, dev))

                if cross:
                    act(ag(2, h, dev))

            @pl.when(z + s < Z)
            def _():
                dev = dev_of(z + s, ys, c)
                if waits:
                    ag(1, h, dev).wait_recv()

                @pl.when(z > 0)
                def _():
                    act(ag(1, h, dev))

                if cross:
                    act(ag(2, h, dev))

    def relays(act, waits):
        @pl.loop(0, PARTS + Z - 2)
        def _(t):
            @pl.loop(1, Z)
            def _(s):
                h = t - (s - 1)

                @pl.when((h >= early) & (h < PARTS))
                def _():
                    relay(h, s, y, Y == 2, act, waits)

                if early:
                    @pl.when((h >= 0) & (h < early))
                    def _():
                        relay(h, s, y, False, act, waits)
                        relay(h, s, 1 - y, False, act, waits)

    crossed(go, True)
    relays(go, True)

    def unfold(shape, a, b):
        p, q = iota(shape, a), iota(shape, b)
        want = (q % folds) * extra + (q // MAIN) * REST + (q % MAIN) // folds
        return (p == want).astype(F32).astype(BF16)

    spread = unfold((rows, rows), 0, 1)
    for h in range(PARTS):
        if Y == 2 and h >= early:
            @pl.loop(0, Z)
            def _(zs):
                for c in range(2):
                    ag(2, h, dev_of(zs, 1 - y, c)).wait_recv()

        @pl.loop(0, devs)
        def _(d):
            Xf[pl.ds(pl.multiple_of(d * MAIN, MAIN), MAIN), :] = X[h, d, :, 0:half]

        got = jnp.dot(
            spread, X[h, :, :, half:].reshape(rows, fold), preferred_element_type=F32
        ).astype(BF16)
        for j in range(folds):
            Xf[rows:, j * fold:(j + 1) * fold] = got[j * extra:(j + 1) * extra]

        @pl.loop(0, nup)
        def _(i):
            if h == 0:
                cup(i).wait()
            a = jnp.dot(Xf[...], wu[i, h * half:(h + 1) * half, :], preferred_element_type=F32)
            at = pl.ds(pl.multiple_of(i * UPC, UPC), UPC)
            if h > 0:
                a += acc_up[:, at]
            if h < PARTS - 1:
                acc_up[:, at] = a
            else:
                hid[:, at] = jax.nn.gelu(a, approximate=True).astype(BF16)

    @pl.loop(0, PARTS)
    def _(h):
        sib(h).wait_send()
        ag_all(h, own, sent)
        ag_all(h, sib_dev, sent)

    crossed(sent, False)
    relays(sent, False)

    def ycopy(h, zd, c):
        return pltpu.make_async_remote_copy(
            X.at[h, dev_of(zd, 1 - y, c)], Yb.at[h, zd, c], y_s.at[h, zd, c], y_r.at[h, zd, c],
            device_id={"cuts": cuts_y},
        )

    def rcopy(h, zd, over, slot, c, tgt):
        ys = 1 - y if over else y
        at = over * 2 + c
        return pltpu.make_async_remote_copy(
            X.at[h, dev_of(zd, ys, c)], Rb.at[h, slot, at], rs_s.at[h, slot, at], rs_r.at[h, slot, at],
            device_id={"cuts": tgt},
        )

    def send_y(h, s):
        for c in range(2):
            @pl.when(z + s < Z)
            def _():
                ycopy(h, z + s, c).start()

            @pl.when((z - s >= 0) & (s > 0))
            def _():
                ycopy(h, z - s, c).start()

    fold_in = unfold((rows, rows), 1, 0)
    for h in range(PARTS):
        @pl.loop(0, per)
        def _(t):
            i = h * per + t
            cdn(i).wait()
            a = jnp.dot(hid[...], wd[i % HELD], preferred_element_type=F32).astype(BF16)

            @pl.when(i + HELD < ndn)
            def _():
                cdn(i + HELD).start()

            X[h, :, :, pl.ds(pl.multiple_of(t * DNC, DNC), DNC)] = a[:rows].reshape(devs, MAIN, DNC)
            for j in range(DNC // fold):
                at = (t * (DNC // fold) + j) * extra
                rcat[pl.ds(pl.multiple_of(at, extra), extra), :] = a[rows:, j * fold:(j + 1) * fold]

        X[h, :, :, half:] = jnp.dot(
            fold_in, rcat[...], preferred_element_type=F32
        ).astype(BF16).reshape(devs, MAIN, fold)
        if Y == 2 and h >= early:
            @pl.loop(0, Z - 2)
            def _(t):
                send_y(h, Z - 1 - t)

    if Y == 2:
        for s in (1, 0):
            @pl.loop(early, PARTS)
            def _(h):
                send_y(h, s)

    def total(h, zd, c, crosses):
        v = X[h, dev_of(zd, y, c)].astype(F32)
        if crosses:
            ycopy(h, zd, c).wait_recv()
            v += Yb[h, zd, c].astype(F32)
        return v

    def arrived(h, over, slot, c):
        rcopy(h, z, over, slot, c, cuts_up).wait_recv()
        return Rb[h, slot, over * 2 + c].astype(F32)

    def fcopy(h):
        return pltpu.make_async_remote_copy(
            fin_out.at[h], fin.at[h, e], fs.at[h], fr.at[h], device_id={"expert": other}
        )

    def hop(h, zd, over, crosses, slot, tgt, opens):
        for c in range(2):
            d = dev_of(zd, 1 - y if over else y, c)
            if crosses:
                v = total(h, zd, c, True)

                @pl.when(opens)
                def _():
                    X[h, d] = v.astype(BF16)

                @pl.when(jnp.logical_not(opens))
                def _():
                    X[h, d] = (v + arrived(h, over, slot, c)).astype(BF16)
            else:
                @pl.when(jnp.logical_not(opens))
                def _():
                    X[h, d] = (X[h, d].astype(F32) + arrived(h, over, slot, c)).astype(BF16)

            rcopy(h, zd, over, slot, c, tgt).start()

    def hops(h, s, over, crosses):
        @pl.when(z + s < Z)
        def _():
            hop(h, z + s, over, crosses, z + s + 1, cuts_up, z == 0)

        @pl.when(z - s >= 0)
        def _():
            hop(h, z - s, over, crosses, z - s, cuts_down, z == Z - 1)

    @pl.loop(0, Z - 1)
    def _(t):
        s = Z - 1 - t
        for h in range(early):
            hops(h, s, 1, False)
            hops(h, s, 0, False)

        @pl.loop(early, PARTS)
        def _(h):
            hops(h, s, 0, Y == 2)

    for h in range(early):
        for c in range(2):
            d = dev_of(z, 1 - y, c)

            @pl.when(z > 0)
            def _():
                X[h, d] = (X[h, d].astype(F32) + arrived(h, 1, z + 1, c)).astype(BF16)

            @pl.when(z < Z - 1)
            def _():
                X[h, d] = (X[h, d].astype(F32) + arrived(h, 1, z, c)).astype(BF16)

            ycopy(h, z, c).start()

    def finish(h):
        for which in range(2):
            c = (other, e)[which]
            dst = fin_out.at[h] if which == 0 else fin.at[h, e]
            dst[...] = total(h, z, c, Y == 2)

            @pl.when(z > 0)
            def _():
                dst[...] += arrived(h, 0, z + 1, c)

            @pl.when(z < Z - 1)
            def _():
                dst[...] += arrived(h, 0, z, c)

            if which == 0:
                fcopy(h).start()

    @pl.loop(early, PARTS)
    def _(h):
        finish(h)

    for h in range(early):
        finish(h)

    q = iota((4 * MAIN, n), 0)
    which = (q // MAIN) % 2
    low = q < 2 * MAIN
    slot = jnp.where(low, q % MAIN, MAIN + (q % MAIN) // folds)
    weight = select(which, slot) * pick(gates, which)
    for h in range(PARTS):
        fcopy(h).wait()
        for j in range(folds):
            lhs = jnp.where(low | (q % folds == j), weight, 0.0)
            rhs = jnp.concatenate(
                [
                    fin[h, :, :, j * fold:(j + 1) * fold].reshape(2 * MAIN, fold),
                    fin[h, :, :, half:].reshape(2 * MAIN, fold),
                ],
                axis=0,
            )
            lo = h * half + j * fold
            out[:, lo:lo + fold] = lax.dot_general(
                lhs, rhs, (((0,), (0,)), ((), ())),
                precision=lax.Precision.HIGHEST, preferred_element_type=F32,
            ).astype(BF16)

    def rs_sent(h, over):
        @pl.loop(1, Z)
        def _(s):
            for c in range(2):
                @pl.when(z + s < Z)
                def _():
                    rcopy(h, z + s, over, z + s + 1, c, cuts_up).wait_send()

                @pl.when(z - s >= 0)
                def _():
                    rcopy(h, z - s, over, z - s, c, cuts_down).wait_send()

    @pl.loop(0, PARTS)
    def _(h):
        rs_sent(h, 0)

    for h in range(early):
        rs_sent(h, 1)
        for c in range(2):
            ycopy(h, z, c).wait_send()

    if Y == 2:
        @pl.loop(early, PARTS)
        def _(h):
            @pl.loop(0, Z)
            def _(zd):
                for c in range(2):
                    ycopy(h, zd, c).wait_send()


def body(Z, Y, tokens, top_experts, gate_fixed, w_up, w_down):
    n, width = tokens.shape
    units = w_up.shape[2]
    half = width // PARTS
    fold = half * REST // MAIN
    devs = 2 * Z * Y
    rows = devs * MAIN
    extra = devs * REST
    nup, ndn = units // UPC, width // DNC
    cols = half + fold
    DMA = pltpu.SemaphoreType.DMA
    vm = pl.BlockSpec(memory_space=pltpu.VMEM)
    anyw = pl.BlockSpec(memory_space=pl.ANY)
    return pl.pallas_call(
        functools.partial(kernel, Z, Y, half, fold),
        out_shape=jax.ShapeDtypeStruct((n, width), BF16),
        in_specs=[vm, vm, vm, anyw, anyw],
        out_specs=vm,
        scratch_shapes=[
            pltpu.VMEM((PARTS, devs, MAIN, cols), BF16),
            pltpu.VMEM((rows + extra, half), BF16),
            pltpu.VMEM((rows + extra, units), F32),
            pltpu.VMEM((rows + extra, units), BF16),
            pltpu.VMEM((nup, width, UPC), BF16),
            pltpu.VMEM((HELD, units, DNC), BF16),
            pltpu.VMEM((PARTS, MAIN, cols), BF16),
            pltpu.VMEM((rows, fold), BF16),
            pltpu.VMEM((PARTS, Z, 2, MAIN, cols), BF16),
            pltpu.VMEM((PARTS, Z + 1, 2 * Y, MAIN, cols), BF16),
            pltpu.VMEM((PARTS, 2, MAIN, cols), F32),
            pltpu.VMEM((PARTS, MAIN, cols), F32),
            DMA((nup,)), DMA((HELD,)),
            DMA((PARTS,)), DMA((PARTS,)),
            DMA((3, PARTS, devs)), DMA((PARTS, devs)),
            DMA((PARTS, Z, 2)), DMA((PARTS, Z, 2)),
            DMA((PARTS, Z + 1, 2 * Y)), DMA((PARTS, Z + 1, 2 * Y)),
            DMA((PARTS,)), DMA((PARTS,)),
        ],
        compiler_params=pltpu.CompilerParams(
            collective_id=0, has_side_effects=True, vmem_limit_bytes=63 * 1024 * 1024
        ),
        cost_estimate=pl.CostEstimate(
            flops=4 * (rows + extra) * width * units,
            bytes_accessed=4 * width * units,
            transcendentals=(rows + extra) * units,
        ),
    )(tokens, top_experts.T, gate_fixed.T, w_up[0], w_down[0])


def solution(mesh):
    cuts = mesh.shape["cuts"]
    Y = 2 if cuts == 8 else 1
    return jax.shard_map(
        functools.partial(body, cuts // Y, Y),
        mesh=mesh,
        in_specs=(
            P(("groups", "expert", "cuts"), None),
            P(("groups", "expert", "cuts"), None),
            P(("groups", "expert", "cuts"), None),
            P("expert", None, "cuts"),
            P("expert", "cuts", None),
        ),
        out_specs=P(("groups", "expert", "cuts"), None),
        check_vma=False,
    )
```

```python
import functools

import jax
import jax.numpy as jnp
from jax import lax
from jax.experimental import pallas as pl
from jax.experimental.pallas import tpu as pltpu
from jax.sharding import PartitionSpec as P

F32, BF16 = jnp.float32, jnp.bfloat16
MAIN = 16
REST = 2
PARTS = 3
FIRST = 0
UPC = 256
DNC = 1024
HELD = 4


def iota(shape, dim):
    return lax.broadcasted_iota(jnp.int32, shape, dim)


def kernel(
    Z, Y, half, fold,
    tok, top, gate, w_up, w_down, out,
    X, Xf, acc_up, hid, wu, wd, stage, rcat, Yb, Rb, fin, fin_out,
    up_sem, dn_sem, sib_s, sib_r, ag_s, ag_r, y_s, y_r, rs_s, rs_r, fs, fr,
):
    e = lax.axis_index("expert")
    k = lax.axis_index("cuts")
    z, y = k // Y, k % Y
    devs = 2 * Z * Y
    rows = devs * MAIN
    extra = devs * REST
    nup, ndn = w_up.shape[1] // UPC, w_down.shape[1] // DNC
    per = ndn // PARTS
    folds = half // fold
    other = 1 - e

    def cup(i):
        return pltpu.make_async_copy(w_up.at[:, pl.ds(i * UPC, UPC)], wu.at[i], up_sem.at[i])

    def cdn(i):
        return pltpu.make_async_copy(
            w_down.at[:, pl.ds(i * DNC, DNC)], wd.at[i % HELD], dn_sem.at[i % HELD]
        )

    barrier = pltpu.get_barrier_semaphore()
    cuts_up, cuts_down, cuts_y = (z + 1) * Y + y, (z - 1) * Y + y, z * Y + (Y - 1 - y)
    pl.semaphore_signal(barrier, inc=1, device_id={"expert": other})
    if Y == 2:
        pl.semaphore_signal(barrier, inc=1, device_id={"cuts": cuts_y})

    @pl.when(z < Z - 1)
    def _():
        pl.semaphore_signal(barrier, inc=1, device_id={"cuts": cuts_up})

    @pl.when(z > 0)
    def _():
        pl.semaphore_signal(barrier, inc=1, device_id={"cuts": cuts_down})

    n = tok.shape[0]
    tri = (iota((n, n), 0) <= iota((n, n), 1)).astype(F32).astype(BF16)
    hits, places, gates = [], [], []
    for x in range(2):
        m = (top[...] == x).astype(F32)
        hit = jnp.sum(m, axis=0, keepdims=True)
        g = jnp.sum(m * (gate[...].astype(F32) * (1.0 / 65536.0)), axis=0, keepdims=True)
        hb = jnp.broadcast_to(hit, (16, n)).astype(BF16)
        places.append(jnp.dot(hb, tri, preferred_element_type=F32)[0:1] - 1.0)
        hits.append(hit)
        gates.append(g)

    def pick(a, which):
        return jnp.where(which == 0, a[0], a[1])

    def select(which, slot):
        at = pick(places, which) == slot.astype(F32)
        return jnp.where(at & (pick(hits, which) > 0.5), 1.0, 0.0)

    ids = iota((MAIN, n), 0)
    mine = iota((MAIN, n), 0) * 0

    def fill(which, h, put):
        w = mine + which
        main = select(w, ids).astype(BF16)
        put(0, half, jnp.dot(main, tok[:, h * half:(h + 1) * half], preferred_element_type=F32).astype(BF16))
        acc = jnp.zeros((MAIN, fold), F32)
        rest = select(w, MAIN + ids // folds)
        for j in range(folds):
            sel = jnp.where(ids % folds == j, rest, 0.0).astype(BF16)
            lo = h * half + j * fold
            acc += jnp.dot(sel, tok[:, lo:lo + fold], preferred_element_type=F32)
        put(half, half + fold, acc.astype(BF16))

    def dev_of(zs, ys, c):
        return (zs * Y + ys) * 2 + c

    def sib(h):
        d = dev_of(z, y, e)
        return pltpu.make_async_remote_copy(
            stage.at[h], X.at[h, d], sib_s.at[h], sib_r.at[h], device_id={"expert": other}
        )

    def ag(d, h, dev):
        tgt = (cuts_up, cuts_down, cuts_y)[d]
        return pltpu.make_async_remote_copy(
            X.at[h, dev], X.at[h, dev], ag_s.at[d, h, dev], ag_r.at[h, dev], device_id={"cuts": tgt}
        )

    def ag_all(h, dev, act):
        @pl.when(z < Z - 1)
        def _():
            act(ag(0, h, dev))

        @pl.when(z > 0)
        def _():
            act(ag(1, h, dev))

        if Y == 2:
            act(ag(2, h, dev))

    def go(c):
        c.start()

    def sent(c):
        c.wait_send()

    own, sib_dev = dev_of(z, y, e), dev_of(z, y, other)
    early = FIRST if Y == 2 else 0

    for h in range(PARTS):
        def put(lo, hi, v):
            stage[h, :, lo:hi] = v

        fill(other, h, put)

    peers = 1 + (1 if Y == 2 else 0) + jnp.where(z < Z - 1, 1, 0) + jnp.where(z > 0, 1, 0)
    pl.semaphore_wait(barrier, peers)

    for h in range(PARTS):
        sib(h).start()
    for h in range(PARTS):
        def put(lo, hi, v):
            X[h, own, :, lo:hi] = v

        fill(e, h, put)
        ag_all(h, own, go)

    @pl.loop(0, PARTS)
    def _(h):
        sib(h).wait_recv()
        ag_all(h, sib_dev, go)

    def along(h, dev, act):
        @pl.when(z < Z - 1)
        def _():
            act(ag(0, h, dev))

        @pl.when(z > 0)
        def _():
            act(ag(1, h, dev))

    def crossed(act, waits):
        for h in range(early):
            for c in range(2):
                dev = dev_of(z, 1 - y, c)
                if waits:
                    ag(2, h, dev).wait_recv()
                along(h, dev, act)

    def relay(h, s, ys, cross, act, waits):
        for c in range(2):
            @pl.when(z - s >= 0)
            def _():
                dev = dev_of(z - s, ys, c)
                if waits:
                    ag(0, h, dev).wait_recv()

                @pl.when(z < Z - 1)
                def _():
                    act(ag(0, h, dev))

                if cross:
                    act(ag(2, h, dev))

            @pl.when(z + s < Z)
            def _():
                dev = dev_of(z + s, ys, c)
                if waits:
                    ag(1, h, dev).wait_recv()

                @pl.when(z > 0)
                def _():
                    act(ag(1, h, dev))

                if cross:
                    act(ag(2, h, dev))

    def relays(act, waits):
        @pl.loop(0, PARTS + Z - 2)
        def _(t):
            @pl.loop(1, Z)
            def _(s):
                h = t - (s - 1)

                @pl.when((h >= early) & (h < PARTS))
                def _():
                    relay(h, s, y, Y == 2, act, waits)

                if early:
                    @pl.when((h >= 0) & (h < early))
                    def _():
                        relay(h, s, y, False, act, waits)
                        relay(h, s, 1 - y, False, act, waits)

    for i in range(nup):
        cup(i).start()
    for i in range(min(HELD, ndn)):
        cdn(i).start()

    crossed(go, True)
    relays(go, True)

    def unfold(shape, a, b):
        p, q = iota(shape, a), iota(shape, b)
        want = (q % folds) * extra + (q // MAIN) * REST + (q % MAIN) // folds
        return (p == want).astype(F32).astype(BF16)

    spread = unfold((rows, rows), 0, 1)
    for h in range(PARTS):
        if Y == 2 and h >= early:
            @pl.loop(0, Z)
            def _(zs):
                for c in range(2):
                    ag(2, h, dev_of(zs, 1 - y, c)).wait_recv()

        @pl.loop(0, devs)
        def _(d):
            Xf[pl.ds(pl.multiple_of(d * MAIN, MAIN), MAIN), :] = X[h, d, :, 0:half]

        got = jnp.dot(
            spread, X[h, :, :, half:].reshape(rows, fold), preferred_element_type=F32
        ).astype(BF16)
        for j in range(folds):
            Xf[rows:, j * fold:(j + 1) * fold] = got[j * extra:(j + 1) * extra]

        @pl.loop(0, nup)
        def _(i):
            if h == 0:
                cup(i).wait()
            a = jnp.dot(Xf[...], wu[i, h * half:(h + 1) * half, :], preferred_element_type=F32)
            at = pl.ds(pl.multiple_of(i * UPC, UPC), UPC)
            if h > 0:
                a += acc_up[:, at]
            if h < PARTS - 1:
                acc_up[:, at] = a
            else:
                hid[:, at] = jax.nn.gelu(a, approximate=True).astype(BF16)

    @pl.loop(0, PARTS)
    def _(h):
        sib(h).wait_send()
        ag_all(h, own, sent)
        ag_all(h, sib_dev, sent)

    crossed(sent, False)
    relays(sent, False)

    def ycopy(h, zd, c):
        return pltpu.make_async_remote_copy(
            X.at[h, dev_of(zd, 1 - y, c)], Yb.at[h, zd, c], y_s.at[h, zd, c], y_r.at[h, zd, c],
            device_id={"cuts": cuts_y},
        )

    def rcopy(h, zd, over, slot, c, tgt):
        ys = 1 - y if over else y
        at = over * 2 + c
        return pltpu.make_async_remote_copy(
            X.at[h, dev_of(zd, ys, c)], Rb.at[h, slot, at], rs_s.at[h, slot, at], rs_r.at[h, slot, at],
            device_id={"cuts": tgt},
        )

    def send_y(h, s):
        for c in range(2):
            @pl.when(z + s < Z)
            def _():
                ycopy(h, z + s, c).start()

            @pl.when((z - s >= 0) & (s > 0))
            def _():
                ycopy(h, z - s, c).start()

    fold_in = unfold((rows, rows), 1, 0)
    for h in range(PARTS):
        @pl.loop(0, per)
        def _(t):
            i = h * per + t
            cdn(i).wait()
            a = jnp.dot(hid[...], wd[i % HELD], preferred_element_type=F32).astype(BF16)

            @pl.when(i + HELD < ndn)
            def _():
                cdn(i + HELD).start()

            X[h, :, :, pl.ds(pl.multiple_of(t * DNC, DNC), DNC)] = a[:rows].reshape(devs, MAIN, DNC)
            for j in range(DNC // fold):
                at = (t * (DNC // fold) + j) * extra
                rcat[pl.ds(pl.multiple_of(at, extra), extra), :] = a[rows:, j * fold:(j + 1) * fold]

        X[h, :, :, half:] = jnp.dot(
            fold_in, rcat[...], preferred_element_type=F32
        ).astype(BF16).reshape(devs, MAIN, fold)
        if Y == 2 and h >= early:
            @pl.loop(0, Z - 2)
            def _(t):
                send_y(h, Z - 1 - t)

    if Y == 2:
        for s in (1, 0):
            @pl.loop(early, PARTS)
            def _(h):
                send_y(h, s)

    def total(h, zd, c, crosses):
        v = X[h, dev_of(zd, y, c)].astype(F32)
        if crosses:
            ycopy(h, zd, c).wait_recv()
            v += Yb[h, zd, c].astype(F32)
        return v

    def arrived(h, over, slot, c):
        rcopy(h, z, over, slot, c, cuts_up).wait_recv()
        return Rb[h, slot, over * 2 + c].astype(F32)

    def fcopy(h):
        return pltpu.make_async_remote_copy(
            fin_out.at[h], fin.at[h, e], fs.at[h], fr.at[h], device_id={"expert": other}
        )

    def hop(h, zd, over, crosses, slot, tgt, opens):
        for c in range(2):
            d = dev_of(zd, 1 - y if over else y, c)
            if crosses:
                v = total(h, zd, c, True)

                @pl.when(opens)
                def _():
                    X[h, d] = v.astype(BF16)

                @pl.when(jnp.logical_not(opens))
                def _():
                    X[h, d] = (v + arrived(h, over, slot, c)).astype(BF16)
            else:
                @pl.when(jnp.logical_not(opens))
                def _():
                    X[h, d] = (X[h, d].astype(F32) + arrived(h, over, slot, c)).astype(BF16)

            rcopy(h, zd, over, slot, c, tgt).start()

    def hops(h, s, over, crosses):
        @pl.when(z + s < Z)
        def _():
            hop(h, z + s, over, crosses, z + s + 1, cuts_up, z == 0)

        @pl.when(z - s >= 0)
        def _():
            hop(h, z - s, over, crosses, z - s, cuts_down, z == Z - 1)

    @pl.loop(0, Z - 1)
    def _(t):
        s = Z - 1 - t
        for h in range(early):
            hops(h, s, 1, False)
            hops(h, s, 0, False)

        @pl.loop(early, PARTS)
        def _(h):
            hops(h, s, 0, Y == 2)

    for h in range(early):
        for c in range(2):
            d = dev_of(z, 1 - y, c)

            @pl.when(z > 0)
            def _():
                X[h, d] = (X[h, d].astype(F32) + arrived(h, 1, z + 1, c)).astype(BF16)

            @pl.when(z < Z - 1)
            def _():
                X[h, d] = (X[h, d].astype(F32) + arrived(h, 1, z, c)).astype(BF16)

            ycopy(h, z, c).start()

    def finish(h):
        for which in range(2):
            c = (other, e)[which]
            dst = fin_out.at[h] if which == 0 else fin.at[h, e]
            dst[...] = total(h, z, c, Y == 2)

            @pl.when(z > 0)
            def _():
                dst[...] += arrived(h, 0, z + 1, c)

            @pl.when(z < Z - 1)
            def _():
                dst[...] += arrived(h, 0, z, c)

            if which == 0:
                fcopy(h).start()

    @pl.loop(early, PARTS)
    def _(h):
        finish(h)

    for h in range(early):
        finish(h)

    q = iota((4 * MAIN, n), 0)
    which = (q // MAIN) % 2
    low = q < 2 * MAIN
    slot = jnp.where(low, q % MAIN, MAIN + (q % MAIN) // folds)
    weight = select(which, slot) * pick(gates, which)
    for h in range(PARTS):
        fcopy(h).wait()
        for j in range(folds):
            lhs = jnp.where(low | (q % folds == j), weight, 0.0)
            rhs = jnp.concatenate(
                [
                    fin[h, :, :, j * fold:(j + 1) * fold].reshape(2 * MAIN, fold),
                    fin[h, :, :, half:].reshape(2 * MAIN, fold),
                ],
                axis=0,
            )
            lo = h * half + j * fold
            out[:, lo:lo + fold] = lax.dot_general(
                lhs, rhs, (((0,), (0,)), ((), ())),
                precision=lax.Precision.HIGHEST, preferred_element_type=F32,
            ).astype(BF16)

    def rs_sent(h, over):
        @pl.loop(1, Z)
        def _(s):
            for c in range(2):
                @pl.when(z + s < Z)
                def _():
                    rcopy(h, z + s, over, z + s + 1, c, cuts_up).wait_send()

                @pl.when(z - s >= 0)
                def _():
                    rcopy(h, z - s, over, z - s, c, cuts_down).wait_send()

    @pl.loop(0, PARTS)
    def _(h):
        rs_sent(h, 0)

    for h in range(early):
        rs_sent(h, 1)
        for c in range(2):
            ycopy(h, z, c).wait_send()

    if Y == 2:
        @pl.loop(early, PARTS)
        def _(h):
            @pl.loop(0, Z)
            def _(zd):
                for c in range(2):
                    ycopy(h, zd, c).wait_send()


def body(Z, Y, tokens, top_experts, gate_fixed, w_up, w_down):
    n, width = tokens.shape
    units = w_up.shape[2]
    half = width // PARTS
    fold = half * REST // MAIN
    devs = 2 * Z * Y
    rows = devs * MAIN
    extra = devs * REST
    nup, ndn = units // UPC, width // DNC
    cols = half + fold
    DMA = pltpu.SemaphoreType.DMA
    vm = pl.BlockSpec(memory_space=pltpu.VMEM)
    anyw = pl.BlockSpec(memory_space=pl.ANY)
    return pl.pallas_call(
        functools.partial(kernel, Z, Y, half, fold),
        out_shape=jax.ShapeDtypeStruct((n, width), BF16),
        in_specs=[vm, vm, vm, anyw, anyw],
        out_specs=vm,
        scratch_shapes=[
            pltpu.VMEM((PARTS, devs, MAIN, cols), BF16),
            pltpu.VMEM((rows + extra, half), BF16),
            pltpu.VMEM((rows + extra, units), F32),
            pltpu.VMEM((rows + extra, units), BF16),
            pltpu.VMEM((nup, width, UPC), BF16),
            pltpu.VMEM((HELD, units, DNC), BF16),
            pltpu.VMEM((PARTS, MAIN, cols), BF16),
            pltpu.VMEM((rows, fold), BF16),
            pltpu.VMEM((PARTS, Z, 2, MAIN, cols), BF16),
            pltpu.VMEM((PARTS, Z + 1, 2 * Y, MAIN, cols), BF16),
            pltpu.VMEM((PARTS, 2, MAIN, cols), F32),
            pltpu.VMEM((PARTS, MAIN, cols), F32),
            DMA((nup,)), DMA((HELD,)),
            DMA((PARTS,)), DMA((PARTS,)),
            DMA((3, PARTS, devs)), DMA((PARTS, devs)),
            DMA((PARTS, Z, 2)), DMA((PARTS, Z, 2)),
            DMA((PARTS, Z + 1, 2 * Y)), DMA((PARTS, Z + 1, 2 * Y)),
            DMA((PARTS,)), DMA((PARTS,)),
        ],
        compiler_params=pltpu.CompilerParams(
            collective_id=0, has_side_effects=True, vmem_limit_bytes=63 * 1024 * 1024
        ),
        cost_estimate=pl.CostEstimate(
            flops=4 * (rows + extra) * width * units,
            bytes_accessed=4 * width * units,
            transcendentals=(rows + extra) * units,
        ),
    )(tokens, top_experts.T, gate_fixed.T, w_up[0], w_down[0])


def solution(mesh):
    cuts = mesh.shape["cuts"]
    Y = 2 if cuts == 8 else 1
    return jax.shard_map(
        functools.partial(body, cuts // Y, Y),
        mesh=mesh,
        in_specs=(
            P(("groups", "expert", "cuts"), None),
            P(("groups", "expert", "cuts"), None),
            P(("groups", "expert", "cuts"), None),
            P("expert", None, "cuts"),
            P("expert", "cuts", None),
        ),
        out_specs=P(("groups", "expert", "cuts"), None),
        check_vma=False,
    )
```
